32 devices in a mesh: dp: 4 (over x, core), cent: 8 (over z, y).
Axes of the slice: x: 2, y: 2, z: 4, core: 2. Of those that a mesh axis runs over, the one named last changes fastest.
Arguments:
- embeddings: bfloat16 [8192, 768], P('dp'), may hold values from -40 to 40
- centroids: float32 [8192, 768], P('cent'), may hold values from -0.5 to 0.5
Outputs:
- new_centroids: float32 [8192, 768], P('cent')
- log_total: float32 [8192], P('dp')
The draws below stay inside these ranges and needn't reach their ends.
All inputs are finite; a program needn't handle non-finite values.
Results may differ from the reference program's by a relative error of at most 0.012.
The reference program's roundings to bfloat16 on the way (of `rounded` and `weights`) count: a program that leaves them out, or rounds other values in their place, can miss the bound.
Values sent between devices are 32-bit elements; how exact they have to be, the bound alone decides.
No kernel may reach another device: no remote copies, remote signals or barrier semaphores. Data moves between devices by JAX's collectives and lax.ppermute only.
A program may use at most 64 MiB of HBM per device.

```python
import jax
import jax.numpy as jnp
from jax import lax

D = 768
KDEV = 1024
R_DEV = 2048
ITERS = 2
K = 8192
ROWS = 8192
N_CENT = 8


logit_divisor = 0.05


def shared_centroids(key, upper):
    key = jax.random.fold_in(key, 101)
    first, second = jax.random.split(key)
    scales = jnp.exp(jax.random.uniform(first, (K, 1), jnp.float32, jnp.log(0.5), jnp.log(upper)))
    base = jax.random.truncated_normal(second, -4.0, 4.0, (K, D), jnp.float32)
    return jnp.clip(base * scales * D ** (-0.5), -0.49, 0.49)


def captured_rows(key, centers, low, high):
    shard_count = ROWS // R_DEV
    first, second, third = jax.random.split(key, 3)
    positions = jnp.arange(ROWS)
    shard = positions // R_DEV
    local = positions % R_DEV
    block_ids = jax.random.randint(first, (shard_count,), 0, K // KDEV)
    orders = jax.vmap(lambda item: jax.random.permutation(item, KDEV))(jax.random.split(second, shard_count))
    chosen = block_ids[shard] * KDEV + orders[shard, local % KDEV]
    heads = centers[chosen]
    pull = jax.random.uniform(third, (ROWS,), jnp.float32, low, high)
    length_energy = jnp.sum(heads * heads, axis=1)
    ratio = 0.5 + logit_divisor * pull / length_energy
    return (ratio[:, None] * heads, local < R_DEV // 2)


def draw_centroids(key, part):
    values = shared_centroids(key, 1.6)
    return jnp.clip(values, -0.5, 0.5)


def draw_embeddings(key, part):
    own_key = jax.random.fold_in(key, 7)
    first, second, third, fourth = jax.random.split(own_key, 4)
    scales = jnp.exp(jax.random.uniform(first, (ROWS, 1), jnp.float32, jnp.log(0.5), jnp.log(5.0)))
    base = jax.random.truncated_normal(second, -4.0, 4.0, (ROWS, D), jnp.float32)
    values = base * scales * D ** (-0.5)
    centers = shared_centroids(key, 1.6)
    copies, taken = captured_rows(fourth, centers, 30.0, 60.0)
    values = jnp.where(taken[:, None], copies, values)
    return values.astype(jnp.bfloat16)


def setup_inputs(seed: int = 0) -> dict:
    keys = jax.random.split(jax.random.key(seed), 3)
    embeddings = draw_embeddings(jax.random.fold_in(keys[2], 71), 0)
    centroids = draw_centroids(jax.random.fold_in(keys[2], 71), 0)
    return dict(embeddings=embeddings, centroids=centroids)


logit_divisor = 0.05
prior = 0.5


def block_scores(embeddings, block):
    rounded = block.astype(jnp.bfloat16)
    pairwise_dots = jnp.dot(embeddings, rounded.T, preferred_element_type=jnp.float32)
    semi_length_energy = 0.5 * jnp.sum(block * block, axis=1)
    return (pairwise_dots - semi_length_energy[None, :]) / logit_divisor


def reference(embeddings, centroids):
    blocks = N_CENT
    width = K // blocks
    current = centroids
    log_total = jnp.zeros((ROWS,), jnp.float32)
    for step in range(ITERS):
        grouped = current.reshape(blocks, width, D)

        def gather_stats(carry, block):
            row_max, row_total = carry
            cluster_logits = block_scores(embeddings, block)
            top = jnp.maximum(row_max, jnp.max(cluster_logits, axis=1))
            row_total = row_total * jnp.exp(row_max - top) + jnp.sum(jnp.exp(cluster_logits - top[:, None]), axis=1)
            return (top, row_total), None

        start = (jnp.full((ROWS,), -jnp.inf, jnp.float32), jnp.zeros((ROWS,), jnp.float32))
        (row_max, row_total), unused = lax.scan(gather_stats, start, grouped)

        def update_block(block):
            cluster_logits = block_scores(embeddings, block)
            weights = (jnp.exp(cluster_logits - row_max[:, None]) / row_total[:, None]).astype(jnp.bfloat16)
            sums = lax.dot_general(weights, embeddings, (((0,), (0,)), ((), ())), preferred_element_type=jnp.float32)
            mass = jnp.sum(weights.astype(jnp.float32), axis=0)
            return (sums + prior * block) / (mass + prior)[:, None]

        current = lax.map(update_block, grouped).reshape(K, D)
        log_total = row_max + jnp.log(row_total)
    return current, log_total
```

```python
import functools

import jax
import jax.numpy as jnp
import numpy as np
from jax import lax
from jax.experimental import pallas as pl
from jax.experimental.pallas import tpu as pltpu
from jax.sharding import PartitionSpec as P

ITERS = 2
UNITS = (1, 2, 1)
CHUNKS = sum(UNITS)
MASS = 8
PARTS = ((1, 4, 3), (1, 4, 3))
EARLY_PARTS = (4, 4)
TAILS = (1, 1)
ROWS = 512
TILE = 256
AHEAD = 3

logit_divisor = 0.05
prior = 0.5
SCALE = float(np.log2(np.e) / logit_divisor)
LN2 = float(np.log(2.0))

ANY = pl.BlockSpec(memory_space=pl.ANY)
VMEM = pl.BlockSpec(memory_space=pltpu.VMEM)
SMEM = pl.BlockSpec(memory_space=pltpu.SMEM)
HBM = pl.BlockSpec(memory_space=pltpu.HBM)


def call(kernel, name, in_specs, out_specs, out_shapes, scratch=(), limit=12, **more):
    return pl.pallas_call(
        kernel,
        in_specs=in_specs,
        out_specs=out_specs,
        out_shape=[jax.ShapeDtypeStruct(s, d) for s, d in out_shapes],
        scratch_shapes=list(scratch),
        compiler_params=pltpu.CompilerParams(vmem_limit_bytes=limit * 2**20),
        cost_estimate=pl.CostEstimate(flops=1, bytes_accessed=1, transcendentals=0),
        name=name,
        **more,
    )


def prepare(c, cb, energy, at):
    n = c.shape[0]
    cb[at : at + n] = c.astype(jnp.bfloat16)
    half = 0.5 * jnp.sum(c * c, axis=1, keepdims=True)
    energy[at : at + n] = jnp.broadcast_to(half, (n, 128))


def score_tile(cb, energy, turned_ref, r, at, size, s_refs):
    rows = slice(r, r + ROWS)
    dots = jnp.dot(cb[at : at + size], turned_ref[:, rows], preferred_element_type=jnp.float32)
    s = (dots - energy[at : at + size, :1]) * SCALE
    n = s_refs[0].shape[0] // 2
    half = len(s_refs) * n
    for k in range(0, size, n):
        side, c = divmod(at + k, half)
        s_refs[c // n][side * n : (side + 1) * n, rows] = s[k : k + n]
    top = jnp.max(s, axis=0, keepdims=True)
    return top, jnp.sum(jnp.exp2(s - top), axis=0, keepdims=True)


def finish_rows(r, parts, stats_ref, prev_ref):
    rows = slice(r, r + ROWS)
    if prev_ref is not None:
        parts = parts + [(prev_ref[0:1, rows], prev_ref[1:2, rows])]
    top = functools.reduce(jnp.maximum, [m for m, _ in parts])
    stats_ref[0:1, rows] = top
    stats_ref[1:2, rows] = sum(l * jnp.exp2(m - top) for m, l in parts)


def first_kernel(core_ref, c_hbm, emb_hbm, emb_ref, turned_ref, stats_ref, *refs):
    s_refs, old_refs = refs[:CHUNKS], refs[CHUNKS : 2 * CHUNKS]
    theirs, cb, energy, c_sems, emb_sems = refs[2 * CHUNKS :]
    n = old_refs[0].shape[0]
    half = CHUNKS * n
    core = core_ref[0]
    starts = [pl.multiple_of(core * half, half), pl.multiple_of((1 - core) * half, half)]
    blocks = range(0, emb_ref.shape[0], ROWS)
    tiles = range(0, 2 * half, TILE)

    def centroids_of(i, at):
        if at >= half:
            to = theirs.at[pl.ds(at - half, TILE)]
            return [pltpu.make_async_copy(c_hbm.at[pl.ds(starts[1] + at - half, TILE)], to, c_sems.at[CHUNKS + i])]
        return [
            pltpu.make_async_copy(c_hbm.at[pl.ds(starts[0] + c * n, n)], old_refs[c], c_sems.at[c])
            for c in range(at // n, (at + TILE) // n)
        ]

    def rows_of(i, r):
        return [pltpu.make_async_copy(emb_hbm.at[pl.ds(r, ROWS)], emb_ref.at[pl.ds(r, ROWS)], emb_sems.at[i])]

    groups = []
    for i in range(max(len(blocks), len(tiles))):
        groups.append((blocks[i : i + 1], [(t, tiles[t]) for t in (i,) if t < len(tiles)]))
    copies = [
        [copy for r in rows for copy in rows_of(i, r)] + [copy for t, at in new for copy in centroids_of(t, at)]
        for i, (rows, new) in enumerate(groups)
    ]
    for group in copies[:AHEAD]:
        for copy in group:
            copy.start()
    have_rows, have_tiles, parts = [], [], {r: [] for r in blocks}
    for i, (new_rows, new_tiles) in enumerate(groups):
        for copy in copies[i]:
            copy.wait()
        for group in copies[i + AHEAD : i + AHEAD + 1]:
            for copy in group:
                copy.start()
        for r in new_rows:
            turned_ref[:, r : r + ROWS] = emb_ref[r : r + ROWS].T
        for _, at in new_tiles:
            if at < half:
                for c in range(at // n, (at + TILE) // n):
                    prepare(old_refs[c][...], cb, energy, c * n)
            else:
                prepare(theirs[at - half : at - half + TILE], cb, energy, at)
        todo = [(r, at) for r in new_rows for at in have_tiles]
        have_rows += new_rows
        todo += [(r, at) for _, at in new_tiles for r in have_rows]
        have_tiles += [at for _, at in new_tiles]
        for r, at in todo:
            parts[r].append(score_tile(cb, energy, turned_ref, r, at, TILE, s_refs))
            if len(parts[r]) == len(tiles):
                finish_rows(r, parts[r], stats_ref, None)


def first_call(core, centroids, embeddings):
    rows, width = embeddings.shape
    count = centroids.shape[0]
    f32, bf16 = jnp.float32, jnp.bfloat16
    emb, turned, stats, *out = call(
        first_kernel, "first_scores", [SMEM, HBM, HBM], [VMEM] * (3 + 2 * CHUNKS),
        [((rows, width), bf16), ((width, rows), bf16), ((2, rows), f32)]
        + [((count // CHUNKS, rows), f32)] * CHUNKS
        + [((count // CHUNKS // 2, width), f32)] * CHUNKS,
        [pltpu.VMEM((count // 2, width), f32), pltpu.VMEM((count, width), bf16), pltpu.VMEM((count, 128), f32),
         pltpu.SemaphoreType.DMA((CHUNKS + count // TILE,)), pltpu.SemaphoreType.DMA((rows // ROWS,))],
        limit=37,
    )(core, centroids, embeddings)
    return out[CHUNKS:], emb, turned, stats, out[:CHUNKS]


def scores_kernel(turned_ref, *refs, chained, chunks, pieces):
    c_refs, refs = refs[:pieces], refs[pieces:]
    prev_ref = refs[0] if chained else None
    stats_ref, *s_refs = refs[chained : chained + 1 + chunks]
    cb, energy = refs[chained + 1 + chunks :]
    at = 0
    for ref in c_refs:
        prepare(ref[...], cb, energy, at)
        at += ref.shape[0]
    for r in range(0, turned_ref.shape[1], ROWS):
        size = min(TILE, cb.shape[0])
        parts = [score_tile(cb, energy, turned_ref, r, at, size, s_refs) for at in range(0, cb.shape[0], size)]
        finish_rows(r, parts, stats_ref, prev_ref)


def scores_call(blocks, chunks, turned, prev):
    width, rows = turned.shape
    total = sum(a.shape[0] for a in blocks)
    chained = prev is not None
    stats, *scores = call(
        functools.partial(scores_kernel, chained=chained, chunks=chunks, pieces=len(blocks)),
        "scores", [VMEM] * (1 + len(blocks) + chained), [VMEM] * (1 + chunks),
        [((2, rows), jnp.float32)] + [((total // chunks, rows), jnp.float32)] * chunks,
        [pltpu.VMEM((total, width), jnp.bfloat16), pltpu.VMEM((total, 128), jnp.float32)],
        limit=24,
    )(turned, *blocks, *([prev] if chained else []))
    return stats, scores


def split(rows, parts):
    tiles = rows // 8
    return [8 * (tiles // parts + (i < tiles % parts)) for i in range(parts)]


def put_rows(refs, at, value):
    done = 0
    for ref in refs:
        size = ref.shape[0]
        n = min(size - at, value.shape[0] - done)
        if at < size and n > 0:
            ref[at : at + n] = value[done : done + n]
            done += n
            at = 0
        else:
            at -= size


def weights_of(s_refs, stats_ref, rows):
    scale = 1.0 / stats_ref[1:2, rows]
    s = jnp.concatenate([ref[:, rows] for ref in s_refs], axis=0)
    return (jnp.exp2(s - stats_ref[0:1, rows]) * scale).astype(jnp.bfloat16)


def lane_sums(w):
    wide = w.astype(jnp.float32)
    return sum(wide[:, at : at + 128] for at in range(0, w.shape[1], 128))


def grouped(refs, counts):
    ends = [sum(counts[: i + 1]) for i in range(len(counts))]
    return [refs[end - count : end] for end, count in zip(ends, counts)]


def sums_kernel(stats_ref, emb_ref, *refs, counts, extra, deps):
    scores, refs = grouped(refs, counts), refs[sum(counts) + deps :]
    out_mine, out_theirs, out_masses = refs[:1], refs[1 : len(refs) - 2 * bool(extra)], refs[-2:]
    n = sum(ref.shape[0] for ref in scores[0]) // 2
    blocks = [slice(r, r + ROWS) for r in range(0, emb_ref.shape[0], ROWS)]
    first, last = (extra[0], len(scores) - extra[1]) if extra else (0, len(scores))
    heavies = []
    for u, s_refs in enumerate(scores):
        acc, heavy = None, None
        for rows in blocks:
            w = weights_of(s_refs, stats_ref, rows)
            if first <= u < last:
                part = jnp.dot(w, emb_ref[rows], preferred_element_type=jnp.float32)
                acc = part if acc is None else acc + part
            if extra:
                heavy = lane_sums(w) if heavy is None else heavy + lane_sums(w)
        if first <= u < last:
            put_rows(out_mine, (u - first) * n, acc[:n])
            put_rows(out_theirs, (u - first) * n, acc[n:])
        heavies.append(heavy)
    if not extra:
        return
    eye = lax.broadcasted_iota(jnp.int32, (n, n), 0) == lax.broadcasted_iota(jnp.int32, (n, n), 1)
    for k, out_ref in enumerate(out_masses):
        out_ref[...] = jnp.zeros_like(out_ref)
        for u, heavy in enumerate(heavies):
            column = jnp.sum(heavy[k * n : (k + 1) * n], axis=1, keepdims=True)
            out_ref[u : u + 1] = jnp.sum(jnp.where(eye, column, 0.0), axis=0, keepdims=True)


def sums_call(scores, extra, stats, embeddings, parts, deps):
    units = len(scores) - sum(extra)
    arrays = [a for unit in scores for a in unit]
    n, width = sum(a.shape[0] for a in scores[0]) // 2, embeddings.shape[1]
    shapes = [(size, width) for size in [units * n] + split(units * n, parts)] + [(MASS, n)] * (2 * bool(extra))
    mine, *out = call(
        functools.partial(sums_kernel, counts=tuple(len(unit) for unit in scores), extra=extra, deps=len(deps)),
        "sums", [VMEM] * (2 + len(arrays)) + [ANY] * len(deps), [VMEM] * len(shapes),
        [(shape, jnp.float32) for shape in shapes],
    )(stats, embeddings, *arrays, *deps)
    return mine, out[:parts], out[parts:]


def side_kernel(stats_ref, emb_ref, s_ref, *refs, side, deps):
    n = s_ref.shape[0] // 2
    acc = None
    for r in range(0, emb_ref.shape[0], ROWS):
        rows = slice(r, r + ROWS)
        w = weights_of([s_ref.at[side * n : (side + 1) * n]], stats_ref, rows)
        part = jnp.dot(w, emb_ref[rows], preferred_element_type=jnp.float32)
        acc = part if acc is None else acc + part
    put_rows(refs[deps:], 0, acc)


def side_call(s, side, stats, embeddings, parts, deps):
    n, width = s.shape[0] // 2, embeddings.shape[1]
    return call(
        functools.partial(side_kernel, side=side, deps=len(deps)),
        "side_sums", [VMEM] * 3 + [ANY] * len(deps), [VMEM] * parts,
        [((size, width), jnp.float32) for size in split(n, parts)],
    )(stats, embeddings, s, *deps)


def fold_kernel(mine_ref, *refs, parts, masses):
    came_refs, mass_refs, total_refs = refs[:parts], refs[parts : parts + masses], refs[parts + masses :]
    at = 0
    for ref in came_refs:
        size = ref.shape[0]
        put_rows(total_refs, at, mine_ref[at : at + size] + ref[...])
        at += size
    if masses:
        total = mass_refs[0][...] + mass_refs[1][...]
        rest = jnp.zeros((MASS, mine_ref.shape[1] - total.shape[1]), jnp.float32)
        put_rows(total_refs, at, jnp.concatenate([total, rest], axis=1))


def fold_call(mine, came, units, masses):
    rows, width = mine.shape
    sizes = [rows // units] * units
    sizes[-1] += MASS * bool(masses)
    return call(
        functools.partial(fold_kernel, parts=len(came), masses=len(masses)),
        "fold", [VMEM] * (1 + len(came) + len(masses)), [VMEM] * units,
        [((size, width), jnp.float32) for size in sizes],
    )(mine, *came, *masses)


def update_kernel(*refs, units, first, whole, deps):
    mass_refs, new_refs = refs[3 * units : 3 * units + 2], refs[3 * units + 2 + deps :]
    n = refs[2].shape[0]
    eye = lax.broadcasted_iota(jnp.int32, (n, n), 0) == lax.broadcasted_iota(jnp.int32, (n, n), 1)
    masses = mass_refs[0][n : n + MASS, :n] + mass_refs[1][n : n + MASS, :n]
    for u in range(units):
        own_ref, far_ref, old_ref = refs[3 * u : 3 * u + 3]
        row = masses[first + u : first + u + 1]
        mass = jnp.sum(jnp.where(eye, row, 0.0), axis=1, keepdims=True)
        new = (own_ref[:n] + far_ref[:n] + prior * old_ref[...]) / (mass + prior)
        if whole:
            new_refs[u][...] = new
        put_rows(new_refs[units * whole :], u * n, new)


def update_call(pieces, masses, old, first, parts, whole, deps):
    units = len(old)
    n, width = old[0].shape
    sizes = [n] * units * whole + (split(units * n, parts) if parts else [])
    out = call(
        functools.partial(update_kernel, units=units, first=first, whole=whole, deps=len(deps)),
        "update", [VMEM] * (3 * units + 2) + [ANY] * len(deps), [VMEM] * len(sizes),
        [((size, width), jnp.float32) for size in sizes],
    )(*[a for p, o in zip(pieces, old) for a in (*p, o)], *masses, *deps)
    return out[: units if whole else None], out[units * whole :] or out


def place_kernel(at_ref, *refs, first, counts, given):
    size = sum(counts)
    blocks, out_ref, done_refs, sems = refs[:size], refs[size + given], refs[size + given + 1 : -1], refs[-1]
    copies = []
    for side, part in enumerate((blocks[: counts[0]], blocks[counts[0] :])):
        at = first
        for ref in part:
            n = ref.shape[0]
            to = out_ref.at[pl.ds(pl.multiple_of(at_ref[side] + at, 8), n)]
            copies.append(pltpu.make_async_copy(ref, to, sems.at[len(copies)]))
            at += n
    for copy in copies:
        copy.start()
    for copy in copies:
        copy.wait()
    for ref in done_refs:
        ref[...] = jnp.zeros_like(ref)


def place_call(at, mine, theirs, first, shape, out):
    given = [] if out is None else [out]
    size = len(mine) + len(theirs)
    done = [((8, 128), jnp.float32)] * (out is None)
    return call(
        functools.partial(place_kernel, first=first, counts=(len(mine), len(theirs)), given=len(given)),
        "place", [SMEM] + [VMEM] * size + [HBM] * len(given), [HBM] + [VMEM] * len(done),
        [(shape, jnp.float32)] + done, [pltpu.SemaphoreType.DMA((size,))],
        input_output_aliases={size + 1: 0} if given else {},
    )(at, *mine, *theirs, *given)


def exchange_stats(stats, n_cent):
    spread = jnp.broadcast_to(stats[None], (n_cent, *stats.shape))
    pairs = lax.all_to_all(spread, "cent", 0, 0)
    top = jnp.max(pairs[:, 0], axis=0)
    total = jnp.sum(jnp.exp2((pairs[:, 0] - top) + jnp.log2(pairs[:, 1])), axis=0)
    return jnp.stack([top, total])


def local(embeddings, centroids, n_dp, n_cent):
    core = lax.axis_index("dp") % 2
    half = centroids.shape[0] // 2
    early = CHUNKS - UNITS[-1]
    firsts = [sum(UNITS[:c]) for c in range(len(UNITS))]
    by_core = lambda a: lax.ppermute(a, "dp", [(i, i ^ 1) for i in range(n_dp)])
    by_chip = lambda a: lax.ppermute(a, "dp", [(i, i ^ 2) for i in range(n_dp)])
    old, embeddings, turned, stats, scores = first_call(core.astype(jnp.int32)[None], centroids, embeddings)
    scores = [(s,) for s in scores]
    for step in range(ITERS):
        last = step == ITERS - 1
        stats = exchange_stats(stats, n_cent)
        log_total = (stats[0] + jnp.log2(stats[1])) * LN2
        sums = []
        for c, (first, units) in enumerate(zip(firsts, UNITS)):
            deps = [sums[-1][0]] if c else []
            deps += [sums[0][1]] if c > 1 else []
            if c == 0:
                theirs, masses = side_call(scores[0][0], 1, stats, embeddings, PARTS[step][0], []), []
                (mine,) = side_call(scores[0][0], 0, stats, embeddings, 1, theirs[-1:])
            elif c == 1:
                extra = (first, CHUNKS - first - units)
                mine, theirs, masses = sums_call(scores, extra, stats, embeddings, PARTS[step][c], deps)
            else:
                mine, theirs, masses = sums_call(scores[first:], (), stats, embeddings, PARTS[step][c], deps)
            masses = [masses[0], by_core(masses[1])] if masses else []
            totals = fold_call(mine, [by_core(t) for t in theirs], units, masses)
            sums += [(t, by_chip(t)) for t in totals]
        masses = sums[early - 1]
        deps = [log_total] if last else []
        new, sent = update_call(sums[:early], masses, old[:early], 0, EARLY_PARTS[step], not last, [sums[-1][0]] + deps)
        came = [by_core(a) for a in sent]
        if last:
            ends = jnp.stack([core * half, (1 - core) * half]).astype(jnp.int32)
            out, ready = place_call(ends, new, came, 0, centroids.shape, None)
        else:
            ready, scores = scores_call([*new, *came], early, turned, None)
            scores = [(s,) for s in scores]
        new_last, sent = update_call(sums[early:], masses, old[early:], early, TAILS[step], not last, [ready])
        came_last = [by_core(a) for a in sent]
        if last:
            (out,) = place_call(ends, new_last, came_last, early * half // CHUNKS, centroids.shape, out)
        else:
            stats, own = scores_call(new_last, 1, turned, ready)
            stats, other = scores_call(came_last, 1, turned, stats)
            scores.append((*own, *other))
            old = new + new_last
    return out, log_total


def solution(mesh):
    n_dp, n_cent = mesh.shape["dp"], mesh.shape["cent"]
    placed = (P("dp", None), P("cent", None))
    return jax.shard_map(
        lambda e, c: local(e, c, n_dp, n_cent),
        mesh=mesh, in_specs=placed, out_specs=(P("cent", None), P("dp")), check_vma=False,
    )
```
